256 devices in a mesh: role: 2 (over z_hi), grp: 4 (over z_lo), tp: 32 (over y, x, core).
Axes of the slice: x: 4, y: 4, z: 8 (z_hi: 2, z_lo: 4; z = z_hi * 4 + z_lo), core: 2. Of those that a mesh axis runs over, the one named last changes fastest.
Arguments:
- hidden: bfloat16 [4, 4, 16384], P(None, 'grp'), may hold values from -6 to 6
- current_weight: bfloat16 [16384, 16384], P(None, ('role', 'tp')), may hold values from -0.046875 to 0.046875
- down_factors: bfloat16 [2, 4, 16384, 64], P('role', 'grp', 'tp'), may hold values from -0.046875 to 0.046875
- up_factors: bfloat16 [2, 4, 64, 16384], P(None, 'grp', None, ('role', 'tp')), may hold values from -0.75 to 0.75
- cache: bfloat16 [4, 8192, 2, 1024], P('grp', ('role', 'tp')), may hold values from -360 to 360
- step_key_value: bfloat16 [4, 4, 2, 1024], P(None, 'grp'), may hold values from -6 to 6
- lengths: int32 [4], P('grp'), may hold values from 1024 to 8192
Outputs:
- attended: bfloat16 [4, 4, 16384], P(None, 'grp', ('role', 'tp'))
The draws below stay inside these ranges and needn't reach their ends.
All inputs are finite; a program needn't handle non-finite values.
Results may differ from the reference program's by a relative error of at most 0.039.
Values may be sent and summed in bfloat16 or wider, within the bound.
No kernel may reach another device: no remote copies, remote signals or barrier semaphores. Data moves between devices by JAX's collectives and lax.ppermute only.
A program may use at most 128 MiB of HBM per device.

```python
import math
import jax
import jax.numpy as jnp
from jax import lax

MODEL_WIDTH = 16384
QUERY_HEADS = 128
KEY_VALUE_HEADS = 8
HEAD_WIDTH = 128
FACTOR_RANK = 64
DECODE_STEPS = 4
ROWS_DEV = 1
TOTAL_ROWS = 4
CACHE_SLOTS = 8192
N_GRP = 4


def draw_cache(key, part):
    key = jax.random.fold_in(key, 11)
    first_product = jax.random.fold_in(key, 0)
    base_matrix = jnp.clip(jax.random.normal(first_product, (TOTAL_ROWS, CACHE_SLOTS, 2, KEY_VALUE_HEADS * HEAD_WIDTH), jnp.float32), -6.0, 6.0)
    return base_matrix.astype(jnp.bfloat16)


def draw_lengths(key, part):
    key = jax.random.fold_in(key, 12)
    first_product, second = jax.random.split(key)
    drawn = jax.random.randint(first_product, (TOTAL_ROWS,), CACHE_SLOTS // 8, CACHE_SLOTS + 1, dtype=jnp.int32)
    longest = jax.random.randint(second, (), 0, TOTAL_ROWS, dtype=jnp.int32)
    return jnp.where(jnp.arange(TOTAL_ROWS, dtype=jnp.int32) == longest, CACHE_SLOTS, drawn).astype(jnp.int32)


def shard_levels(own_key, extent, cuts, low, top_value):
    loudness, own = 1.0, jax.random.fold_in(own_key, 6)
    for dim, shards_of in cuts:
        draws = jnp.exp(jax.random.uniform(jax.random.fold_in(own, dim), (shards_of,), jnp.float32, low / len(cuts), top_value / len(cuts)))
        loudness = loudness * jnp.repeat(draws, extent[dim] // shards_of).reshape([-1 if axis == dim else 1 for axis in range(len(extent))])
    return loudness


def gaussian(key, shape, deviation, limit, pieces=(), held_as=jnp.bfloat16):
    level = shard_levels(key, shape, pieces, -0.22, 0.18) if pieces else 1.0
    result = jax.random.normal(key, shape, jnp.float32) * deviation * level
    return jnp.minimum(jnp.maximum(result, -limit), limit).astype(held_as)


def setup_inputs(seed: int = 0) -> dict:
    splits = jax.random.split(jax.random.key(seed), 8)
    hidden = gaussian(splits[0], (DECODE_STEPS, TOTAL_ROWS, MODEL_WIDTH), 1.0, 6.0, ((1, 4),))
    current_weight = gaussian(splits[1], (MODEL_WIDTH, QUERY_HEADS * HEAD_WIDTH), MODEL_WIDTH ** -0.5, 0.046875, ((1, 64),))
    down_factors = gaussian(splits[2], (2, N_GRP, MODEL_WIDTH, FACTOR_RANK), MODEL_WIDTH ** -0.5, 0.046875, ((0, 2), (1, 4), (2, 32)))
    up_factors = gaussian(splits[3], (2, N_GRP, FACTOR_RANK, QUERY_HEADS * HEAD_WIDTH), FACTOR_RANK ** -0.5, 0.75, ((1, 4), (3, 64)))
    cache = draw_cache(jax.random.fold_in(splits[7], 71), 0)
    step_key_value = gaussian(splits[5], (DECODE_STEPS, TOTAL_ROWS, 2, KEY_VALUE_HEADS * HEAD_WIDTH), 1.0, 6.0, ((1, 4),))
    lengths = draw_lengths(jax.random.fold_in(splits[7], 71), 0)
    return dict(hidden=hidden, current_weight=current_weight, down_factors=down_factors, up_factors=up_factors, cache=cache, step_key_value=step_key_value, lengths=lengths)


def rotate(vec, pos):
    half = vec.shape[-1] // 2
    freq = jnp.exp(jnp.arange(half, dtype=jnp.float32) * (-2.0 * math.log(500000.0) / vec.shape[-1]))
    angle = pos.astype(jnp.float32)[..., None, None] * freq
    cosine = jnp.cos(angle)
    sine = jnp.sin(angle)
    first_product = vec[..., :half]
    second = vec[..., half:]
    return jnp.concatenate([first_product * cosine - second * sine, second * cosine + first_product * sine], axis=-1)

def reference(hidden, current_weight, down_factors, up_factors, cache, step_key_value, lengths):
    cols = QUERY_HEADS * HEAD_WIDTH
    groups = []
    for group_index in range(N_GRP):
        left_factor = jnp.concatenate([down_factors[0, group_index], -down_factors[1, group_index]], axis=1)
        right_factor = jnp.concatenate([up_factors[0, group_index], up_factors[1, group_index]], axis=0).astype(jnp.float32)
        rows_in = hidden[:, group_index * ROWS_DEV:(group_index + 1) * ROWS_DEV].reshape(DECODE_STEPS * ROWS_DEV, MODEL_WIDTH)
        low = jnp.dot(rows_in, left_factor, preferred_element_type=jnp.float32)
        base_matrix = jnp.dot(rows_in, current_weight, preferred_element_type=jnp.float32)
        extra = jnp.dot(low, right_factor, precision=lax.Precision.HIGHEST)
        groups.append((base_matrix + extra).reshape(DECODE_STEPS, ROWS_DEV, cols))
    raw = jnp.concatenate(groups, axis=1).reshape(DECODE_STEPS, TOTAL_ROWS, QUERY_HEADS, HEAD_WIDTH)
    steps_pos = lengths[None, :] + jnp.arange(DECODE_STEPS, dtype=jnp.int32)[:, None]
    query_vector = rotate(raw, steps_pos).astype(jnp.bfloat16)
    newest_token = step_key_value[:, :, 0].reshape(DECODE_STEPS, TOTAL_ROWS, KEY_VALUE_HEADS, HEAD_WIDTH).astype(jnp.float32)
    fresh_key = rotate(newest_token, steps_pos).astype(jnp.bfloat16).astype(jnp.float32)
    newest_value = step_key_value[:, :, 1].reshape(DECODE_STEPS, TOTAL_ROWS, KEY_VALUE_HEADS, HEAD_WIDTH).astype(jnp.float32)
    key_rows = cache[:, :, 0].reshape(TOTAL_ROWS, CACHE_SLOTS, KEY_VALUE_HEADS, HEAD_WIDTH).astype(jnp.float32)
    value_rows = cache[:, :, 1].reshape(TOTAL_ROWS, CACHE_SLOTS, KEY_VALUE_HEADS, HEAD_WIDTH).astype(jnp.float32)
    valid = (jnp.arange(CACHE_SLOTS, dtype=jnp.int32)[None, :] < lengths[:, None])[:, None, None, :]
    scale = 1.0 / math.sqrt(HEAD_WIDTH)
    group_share = QUERY_HEADS // KEY_VALUE_HEADS
    results = []
    for step_index in range(DECODE_STEPS):
        grouped_queries = query_vector[step_index].astype(jnp.float32).reshape(TOTAL_ROWS, KEY_VALUE_HEADS, group_share, HEAD_WIDTH)
        scores = jnp.einsum('rgqd,rpgd->rgqp', grouped_queries, key_rows) * scale
        fresh_scores = jnp.einsum('rgqd,srgd->rgqs', grouped_queries, fresh_key) * scale
        fresh_ok = (jnp.arange(DECODE_STEPS) <= step_index)[None, None, None, :]
        top = jnp.maximum(lax.optimization_barrier(jnp.max(jnp.where(valid, scores, -1e+30), axis=-1)), lax.optimization_barrier(jnp.max(jnp.where(fresh_ok, fresh_scores, -1e+30), axis=-1)))
        weights = jnp.where(valid, jnp.exp(scores - top[..., None]), 0.0)
        fresh_w = jnp.where(fresh_ok, jnp.exp(fresh_scores - top[..., None]), 0.0)
        total = lax.optimization_barrier(jnp.sum(weights, axis=-1)) + lax.optimization_barrier(jnp.sum(fresh_w, axis=-1))
        summed = jnp.einsum('rgqp,rpgd->rgqd', weights, value_rows) + jnp.einsum('rgqs,srgd->rgqd', fresh_w, newest_value)
        results.append((summed / total[..., None]).reshape(TOTAL_ROWS, QUERY_HEADS * HEAD_WIDTH).astype(jnp.bfloat16))
    return jnp.stack(results, axis=0)
```

```python
import math

import jax
import jax.numpy as jnp
from jax import lax
from jax.experimental import pallas as pl
from jax.experimental.pallas import tpu as pltpu
from jax.sharding import Mesh, PartitionSpec as P

QUERY_HEADS = 128
KEY_VALUE_HEADS = 8
HEAD_WIDTH = 128
DECODE_STEPS = 4
BLOCK_X = 4
BLOCK_CORE = 2
BLOCK = BLOCK_X * BLOCK_CORE
SHARE = QUERY_HEADS // KEY_VALUE_HEADS
ROWS = SHARE * DECODE_STEPS
MASKED = -1e30


def rotate(vec, pos):
    half = vec.shape[-1] // 2
    freq = jnp.exp(
        jnp.arange(half, dtype=jnp.float32) * (-2.0 * math.log(500000.0) / vec.shape[-1])
    )
    angle = pos.astype(jnp.float32)[..., None, None] * freq
    cosine = jnp.cos(angle)
    sine = jnp.sin(angle)
    first = vec[..., :half]
    second = vec[..., half:]
    turned = jnp.concatenate(
        [first * cosine - second * sine, second * cosine + first * sine], axis=-1
    )
    return turned, cosine, sine


def attend_kernel(info, lows, base, up, turn, cached, fresh, out, query):
    low = jnp.sum(lows[...], axis=0)
    high = low.astype(jnp.bfloat16).astype(jnp.float32)
    rest = low - high
    middle = rest.astype(jnp.bfloat16).astype(jnp.float32)
    terms = jnp.concatenate([high, middle, rest - middle, jnp.zeros_like(low)], axis=0).astype(
        jnp.bfloat16
    )
    cosine = turn[0]
    sine = turn[1]
    for j in range(BLOCK):
        extra = jnp.dot(terms, up[j], preferred_element_type=jnp.float32)
        raw = base[j] + ((extra[8:12] + extra[4:8]) + extra[0:4])
        for i in range(2):
            head = raw[:, i * HEAD_WIDTH : (i + 1) * HEAD_WIDTH]
            row = (2 * j + i) * DECODE_STEPS
            query[row : row + DECODE_STEPS, :] = head * cosine + pltpu.roll(head, 64, 1) * sine
    queries = query[...].astype(jnp.bfloat16)
    scale = 1.0 / math.sqrt(HEAD_WIDTH)
    length = info[0]
    place = info[1]
    n_src, pairs, _ = cached.shape
    column = lax.broadcasted_iota(jnp.int32, (ROWS, pairs), 1)
    row = lax.broadcasted_iota(jnp.int32, (ROWS, HEAD_WIDTH), 0)
    lane = lax.broadcasted_iota(jnp.int32, (ROWS, HEAD_WIDTH), 1)
    keyed = lax.rem(column, 2) == 0
    position = lax.div(column, 2)
    contract = (((1,), (1,)), ((), ()))
    masks = []
    scores = []
    for j in range(n_src):
        s = lax.dot_general(queries, cached[j], contract, preferred_element_type=jnp.float32)
        start = (j * BLOCK + place) * (pairs // 2)
        ok = keyed & (position + start < length)
        masks.append(ok)
        scores.append(jnp.where(ok, s * scale, MASKED))
    s = lax.dot_general(queries, fresh[...], contract, preferred_element_type=jnp.float32)
    ok = (lax.rem(lane, 2) == 0) & (lax.div(lane, 2) <= lax.rem(row, DECODE_STEPS)) & (place == 0)
    masks.append(ok)
    scores.append(jnp.where(ok, s * scale, MASKED))
    top = jnp.max(scores[-1], axis=-1, keepdims=True)
    for s in scores[:-1]:
        top = jnp.maximum(top, jnp.max(s, axis=-1, keepdims=True))
    total = jnp.zeros_like(top)
    summed = jnp.zeros((ROWS, HEAD_WIDTH), jnp.float32)
    for j in range(n_src + 1):
        weight = jnp.where(masks[j], jnp.exp(scores[j] - top), 0.0)
        total = total + jnp.sum(weight, axis=-1, keepdims=True)
        values = cached[j] if j < n_src else fresh[...]
        summed = summed + jnp.dot(
            pltpu.roll(weight, 1, 1).astype(jnp.bfloat16), values, preferred_element_type=jnp.float32
        )
    stats = jnp.where(lane < 64, top, total)
    each = 2 * DECODE_STEPS
    for d in range(BLOCK):
        out[d, :each, :] = summed[d * each : (d + 1) * each, :]
        out[d, each:, :] = stats[d * each : (d + 1) * each, :]


def combine_kernel(parts, out):
    each = 2 * DECODE_STEPS
    tops = [parts[d, each:, :][:, 0:1] for d in range(BLOCK)]
    totals = [parts[d, each:, :][:, 64:65] for d in range(BLOCK)]
    top = tops[0]
    for d in range(1, BLOCK):
        top = jnp.maximum(top, tops[d])
    total = jnp.zeros_like(top)
    summed = jnp.zeros((each, HEAD_WIDTH), jnp.float32)
    for d in range(BLOCK):
        factor = jnp.exp(tops[d] - top)
        total = total + totals[d] * factor
        summed = summed + parts[d, :each, :] * factor
    whole = summed / total
    out[...] = jnp.concatenate([whole[:DECODE_STEPS], whole[DECODE_STEPS:]], axis=1).astype(
        jnp.bfloat16
    )


def local(hidden, current_weight, down_factors, up_factors, cache, step_key_value, lengths):
    plane = ("y", "x", "core")
    block = ("x", "core")
    side = lax.axis_index("role")
    shard = lax.axis_index(plane)
    place = lax.axis_index(block)
    key_head = lax.axis_index(("role", "y"))
    rows = hidden.reshape(DECODE_STEPS, -1)
    down = down_factors[0, 0]
    part = jnp.dot(
        lax.dynamic_slice_in_dim(rows, shard * down.shape[0], down.shape[0], 1),
        down,
        preferred_element_type=jnp.float32,
    )
    blank = jnp.zeros_like(part)
    part = jnp.where(
        side == 0,
        jnp.concatenate([part, blank], axis=1),
        jnp.concatenate([blank, -part], axis=1),
    )
    everyone = ("role",) + plane
    lows = lax.all_to_all(
        jnp.broadcast_to(part, (lax.axis_size(everyone),) + part.shape), everyone, 0, 0
    )

    pairs = cache.shape[1] * 2
    sent = cache.reshape(pairs, KEY_VALUE_HEADS, HEAD_WIDTH).transpose(1, 0, 2)
    cached = lax.all_to_all(sent, ("role", "y"), 0, 0)

    up = up_factors.reshape(-1, up_factors.shape[-1])
    up = lax.all_to_all(jnp.broadcast_to(up, (BLOCK,) + up.shape), block, 0, 0)

    base = jnp.dot(rows, current_weight, preferred_element_type=jnp.float32)
    base = lax.all_to_all(jnp.broadcast_to(base, (BLOCK,) + base.shape), block, 0, 0)

    steps_pos = lengths[None, :] + jnp.arange(DECODE_STEPS, dtype=jnp.int32)[:, None]
    own = lax.dynamic_slice_in_dim(step_key_value, key_head * HEAD_WIDTH, HEAD_WIDTH, 3)
    fresh_key, cosine, sine = rotate(own[:, :, 0][:, :, None].astype(jnp.float32), steps_pos)
    cosine, sine = cosine[:, 0, 0], sine[:, 0, 0]
    turn = jnp.stack(
        [
            jnp.concatenate([cosine, cosine], axis=-1),
            jnp.concatenate([-sine, sine], axis=-1),
        ]
    )
    fresh = jnp.stack([fresh_key[:, 0, 0].astype(jnp.bfloat16), own[:, 0, 1]], axis=1)
    fresh = jnp.pad(
        fresh.reshape(2 * DECODE_STEPS, HEAD_WIDTH), ((0, HEAD_WIDTH - 2 * DECODE_STEPS), (0, 0))
    )
    info = jnp.concatenate([lengths, place[None].astype(jnp.int32)])

    vmem = pl.BlockSpec(memory_space=pltpu.VMEM)
    parts = pl.pallas_call(
        attend_kernel,
        out_shape=jax.ShapeDtypeStruct((BLOCK, 4 * DECODE_STEPS, HEAD_WIDTH), jnp.float32),
        in_specs=[pl.BlockSpec(memory_space=pltpu.SMEM)] + [vmem] * 6,
        out_specs=vmem,
        scratch_shapes=[pltpu.VMEM((ROWS, HEAD_WIDTH), jnp.float32)],
        compiler_params=pltpu.CompilerParams(vmem_limit_bytes=16 * 2**20),
        name="attend",
    )(info, lows, base, up, turn, cached, fresh)
    parts = lax.all_to_all(parts, block, 0, 0)
    out = pl.pallas_call(
        combine_kernel,
        out_shape=jax.ShapeDtypeStruct((DECODE_STEPS, 2 * HEAD_WIDTH), jnp.bfloat16),
        in_specs=[vmem],
        out_specs=vmem,
        name="combine",
    )(parts)
    return out[:, None, :]


def solution(mesh):
    role, grp, tp = mesh.devices.shape
    finer = Mesh(
        mesh.devices.reshape(role, grp, tp // BLOCK, BLOCK_X, BLOCK_CORE),
        ("role", "grp", "y", "x", "core"),
    )
    tp = ("y", "x", "core")
    both = ("role",) + tp
    placed = (
        P(None, "grp", None),
        P(None, both),
        P("role", "grp", tp, None),
        P(None, "grp", None, both),
        P("grp", both, None, None),
        P(None, "grp", None, None),
        P("grp"),
    )
    return jax.shard_map(
        local, mesh=finer, in_specs=placed, out_specs=P(None, "grp", both), check_vma=False
    )
```

```python
import math

import jax
import jax.numpy as jnp
from jax import lax
from jax.experimental import pallas as pl
from jax.experimental.pallas import tpu as pltpu
from jax.sharding import Mesh, PartitionSpec as P

QUERY_HEADS = 128
KEY_VALUE_HEADS = 8
HEAD_WIDTH = 128
DECODE_STEPS = 4
BLOCK_X = 4
BLOCK_CORE = 2
BLOCK = BLOCK_X * BLOCK_CORE
SHARE = QUERY_HEADS // KEY_VALUE_HEADS
ROWS = SHARE * DECODE_STEPS
MASKED = -1e30


def angles(pos):
    half = HEAD_WIDTH // 2
    freq = jnp.exp(
        jnp.arange(half, dtype=jnp.float32) * (-2.0 * math.log(500000.0) / HEAD_WIDTH)
    )
    angle = pos.astype(jnp.float32)[:, None] * freq
    return jnp.cos(angle), jnp.sin(angle)


def swapped(block, axis, apart):
    count = lax.axis_size(axis)
    return lax.ppermute(block, axis, [(i, i ^ apart) for i in range(count)])


def split_kernel(info, hidden, down, cache, out):
    depth = down.shape[1]
    own = pl.ds(pl.multiple_of(info[0] * depth, depth), depth)
    part = lax.dot_general(
        hidden[:, own], down[...], (((1,), (1,)), ((), ())), preferred_element_type=jnp.float32
    )
    high = part.astype(jnp.bfloat16).astype(jnp.float32)
    middle = (part - high).astype(jnp.bfloat16).astype(jnp.float32)
    rest = part - high - middle
    terms = jnp.concatenate([high, middle], axis=1).astype(jnp.bfloat16)
    others = jnp.concatenate([rest, jnp.zeros_like(rest)], axis=1).astype(jnp.bfloat16)
    positions = cache.shape[0]
    for head in range(KEY_VALUE_HEADS):
        out[head, :positions] = cache[:, :, head * HEAD_WIDTH : (head + 1) * HEAD_WIDTH]
        out[head, positions:, 0, :] = terms
        out[head, positions:, 1, :] = others


def attend_kernel(info, message, up0, up1, up2, up3, turn, cached, newest, out, query):
    ups = (up0, up1, up2, up3)
    length = info[0]
    place = info[1]
    rank = up0.shape[0] // BLOCK_CORE
    low = jnp.sum(message[:, :, :rank], axis=0)
    high = low.astype(jnp.bfloat16).astype(jnp.float32)
    rest = low - high
    middle = rest.astype(jnp.bfloat16).astype(jnp.float32)
    terms = jnp.concatenate([high, middle, rest - middle, jnp.zeros_like(low)], axis=0).astype(
        jnp.bfloat16
    )
    cosine = turn[0]
    sine = turn[1]
    for j in range(BLOCK):
        up = ups[j // BLOCK_CORE][(j % BLOCK_CORE) * rank : (j % BLOCK_CORE + 1) * rank, :]
        extra = jnp.dot(terms, up, preferred_element_type=jnp.float32)
        raw = message[place ^ j][:, rank:] + ((extra[8:12] + extra[4:8]) + extra[0:4])
        for i in range(2):
            head = raw[:, i * HEAD_WIDTH : (i + 1) * HEAD_WIDTH]
            row = (2 * j + i) * DECODE_STEPS
            query[row : row + DECODE_STEPS, :] = head * cosine + pltpu.roll(head, 64, 1) * sine
    queries = query[...].astype(jnp.bfloat16)
    scale = 1.0 / math.sqrt(HEAD_WIDTH)
    own = pl.ds(pl.multiple_of(info[2] * HEAD_WIDTH, HEAD_WIDTH), HEAD_WIDTH)
    token = newest[:, 0, 0, own].astype(jnp.float32)
    token = token * cosine + pltpu.roll(token, 64, 1) * sine
    blank = jnp.zeros((HEAD_WIDTH - DECODE_STEPS, HEAD_WIDTH), jnp.float32)
    fresh_key = jnp.concatenate([token, blank], axis=0).astype(jnp.bfloat16)
    fresh_value = jnp.concatenate(
        [newest[:, 0, 1, own].astype(jnp.float32), blank], axis=0
    ).astype(jnp.bfloat16)
    n_src = cached.shape[0]
    pairs = cached.shape[1] - 2 * DECODE_STEPS
    column = lax.broadcasted_iota(jnp.int32, (ROWS, pairs), 1)
    row = lax.broadcasted_iota(jnp.int32, (ROWS, HEAD_WIDTH), 0)
    lane = lax.broadcasted_iota(jnp.int32, (ROWS, HEAD_WIDTH), 1)
    keyed = lax.rem(column, 2) == 0
    position = lax.div(column, 2)
    contract = (((1,), (1,)), ((), ()))
    masks = []
    scores = []
    for j in range(n_src):
        s = lax.dot_general(queries, cached[j, :pairs, :], contract, preferred_element_type=jnp.float32)
        start = (j * BLOCK + place) * (pairs // 2)
        ok = keyed & (position + start < length)
        masks.append(ok)
        scores.append(jnp.where(ok, s * scale, MASKED))
    s = lax.dot_general(queries, fresh_key, contract, preferred_element_type=jnp.float32)
    ok = (lane <= lax.rem(row, DECODE_STEPS)) & (place == 0)
    masks.append(ok)
    scores.append(jnp.where(ok, s * scale, MASKED))
    top = jnp.max(scores[-1], axis=-1, keepdims=True)
    for s in scores[:-1]:
        top = jnp.maximum(top, jnp.max(s, axis=-1, keepdims=True))
    total = jnp.zeros_like(top)
    summed = jnp.zeros((ROWS, HEAD_WIDTH), jnp.float32)
    for j in range(n_src + 1):
        weight = jnp.where(masks[j], jnp.exp(scores[j] - top), 0.0)
        total = total + jnp.sum(weight, axis=-1, keepdims=True)
        if j < n_src:
            weight, values = pltpu.roll(weight, 1, 1), cached[j, :pairs, :]
        else:
            values = fresh_value
        summed = summed + jnp.dot(
            weight.astype(jnp.bfloat16), values, preferred_element_type=jnp.float32
        )
    stats = jnp.where(lane < 64, top, total)
    each = 2 * DECODE_STEPS
    for d in range(BLOCK):
        out[place ^ d, :each, :] = summed[d * each : (d + 1) * each, :]
        out[place ^ d, each:, :] = stats[d * each : (d + 1) * each, :]


def combine(parts):
    each = 2 * DECODE_STEPS
    summed, stats = parts[:, :each], parts[:, each:]
    tops, totals = stats[:, :, :1], stats[:, :, 64:65]
    factor = jnp.exp(tops - jnp.max(tops, axis=0, keepdims=True))
    whole = jnp.sum(summed * factor, axis=0) / jnp.sum(totals * factor, axis=0)
    whole = whole.reshape(2, DECODE_STEPS, HEAD_WIDTH).swapaxes(0, 1)
    return whole.reshape(DECODE_STEPS, 2 * HEAD_WIDTH).astype(jnp.bfloat16)


def local(hidden, current_weight, down_factors, up_factors, cache, step_key_value, lengths):
    plane = ("y", "x", "core")
    block = ("x", "core")
    shard = lax.axis_index(plane)
    place = lax.axis_index(block)
    key_head = lax.axis_index(("role", "y"))
    rows = hidden.reshape(DECODE_STEPS, -1)
    down = down_factors[0, 0].T
    vmem = pl.BlockSpec(memory_space=pltpu.VMEM)
    smem = pl.BlockSpec(memory_space=pltpu.SMEM)
    positions = cache.shape[1]
    sent = pl.pallas_call(
        split_kernel,
        out_shape=jax.ShapeDtypeStruct(
            (KEY_VALUE_HEADS, positions + DECODE_STEPS, 2, HEAD_WIDTH), cache.dtype
        ),
        in_specs=[smem] + [vmem] * 3,
        out_specs=vmem,
        name="split",
    )(shard[None].astype(jnp.int32), rows, down, cache[0])
    cached = lax.all_to_all(sent, ("role", "y"), 0, 0)
    terms = cached[:, positions:].astype(jnp.float32)
    rank = down.shape[0]
    terms = (terms[:, :, 1, :rank] + terms[:, :, 0, rank:]) + terms[:, :, 0, :rank]
    terms = jnp.sum(terms.reshape(2, -1, DECODE_STEPS, rank), axis=1)
    low = jnp.concatenate([terms[0], -terms[1]], axis=1)
    cached = cached.reshape(KEY_VALUE_HEADS, -1, HEAD_WIDTH)

    up = up_factors.reshape(-1, up_factors.shape[-1])
    up = jnp.concatenate([up, swapped(up, "core", 1)], axis=0)
    ups = [up] + [swapped(up, "x", m) for m in range(1, BLOCK_X)]

    base = jnp.dot(rows, current_weight, preferred_element_type=jnp.float32)
    message = jnp.concatenate([low, base], axis=1)
    message = lax.all_to_all(jnp.broadcast_to(message, (BLOCK,) + message.shape), block, 0, 0)

    steps_pos = lengths[None, :] + jnp.arange(DECODE_STEPS, dtype=jnp.int32)[:, None]
    cosine, sine = angles(steps_pos[:, 0])
    turn = jnp.stack(
        [
            jnp.concatenate([cosine, cosine], axis=-1),
            jnp.concatenate([-sine, sine], axis=-1),
        ]
    )
    info = jnp.stack([lengths[0], place, key_head]).astype(jnp.int32)

    parts = pl.pallas_call(
        attend_kernel,
        out_shape=jax.ShapeDtypeStruct((BLOCK, 4 * DECODE_STEPS, HEAD_WIDTH), jnp.float32),
        in_specs=[smem] + [vmem] * 8,
        out_specs=vmem,
        scratch_shapes=[pltpu.VMEM((ROWS, HEAD_WIDTH), jnp.float32)],
        compiler_params=pltpu.CompilerParams(vmem_limit_bytes=16 * 2**20),
        name="attend",
    )(info, message, *ups, turn, cached, step_key_value)
    parts = lax.all_to_all(parts, block, 0, 0)
    out = combine(parts)
    return out[:, None, :]


def solution(mesh):
    role, grp, tp = mesh.devices.shape
    finer = Mesh(
        mesh.devices.reshape(role, grp, tp // BLOCK, BLOCK_X, BLOCK_CORE),
        ("role", "grp", "y", "x", "core"),
    )
    tp = ("y", "x", "core")
    both = ("role",) + tp
    placed = (
        P(None, "grp", None),
        P(None, both),
        P("role", "grp", tp, None),
        P(None, "grp", None, both),
        P("grp", both, None, None),
        P(None, "grp", None, None),
        P("grp"),
    )
    return jax.shard_map(
        local, mesh=finer, in_specs=placed, out_specs=P(None, "grp", both), check_vma=False
    )
```

```python
import math

import jax
import jax.numpy as jnp
from jax import lax
from jax.experimental import pallas as pl
from jax.experimental.pallas import tpu as pltpu
from jax.sharding import Mesh, PartitionSpec as P

QUERY_HEADS = 128
KEY_VALUE_HEADS = 8
HEAD_WIDTH = 128
DECODE_STEPS = 4
BLOCK_X = 4
BLOCK_CORE = 2
BLOCK = BLOCK_X * BLOCK_CORE
SHARE = QUERY_HEADS // KEY_VALUE_HEADS
ROWS = SHARE * DECODE_STEPS
MASKED = -1e30


def angles(pos):
    half = HEAD_WIDTH // 2
    freq = jnp.exp(
        jnp.arange(half, dtype=jnp.float32) * (-2.0 * math.log(500000.0) / HEAD_WIDTH)
    )
    angle = pos.astype(jnp.float32)[:, None] * freq
    return jnp.cos(angle), jnp.sin(angle)


def swapped(block, axis, apart):
    count = lax.axis_size(axis)
    return lax.ppermute(block, axis, [(i, i ^ apart) for i in range(count)])


SPLITS = 4


def split_kernel(info, hidden, down, cache, out, some, factor, held, ready, sems):
    positions = cache.shape[0]
    piece = positions // SPLITS
    depth = down.shape[1]
    own = pl.ds(pl.multiple_of(info[0] * depth, depth), depth)
    fetches = [
        pltpu.make_async_copy(hidden.at[:, own], some, sems.at[0]),
        pltpu.make_async_copy(down, factor, sems.at[1]),
    ]
    for k in range(SPLITS):
        rows = pl.ds(k * piece, piece)
        fetches.append(pltpu.make_async_copy(cache.at[rows], held.at[rows], sems.at[2 + k]))
    for fetch in fetches:
        fetch.start()
    stores = []
    for k in range(SPLITS):
        fetches[2 + k].wait()
        rows = slice(k * piece, (k + 1) * piece)
        for head in range(KEY_VALUE_HEADS):
            columns = slice(head * HEAD_WIDTH, (head + 1) * HEAD_WIDTH)
            ready[head, rows] = held[rows, :, columns]
        rows = pl.ds(k * piece, piece)
        stores.append(
            pltpu.make_async_copy(ready.at[:, rows], out.at[:, rows], sems.at[2 + SPLITS + k])
        )
        stores[-1].start()
    fetches[0].wait()
    fetches[1].wait()
    part = lax.dot_general(
        some[...], factor[...], (((1,), (1,)), ((), ())), preferred_element_type=jnp.float32
    )
    high = part.astype(jnp.bfloat16).astype(jnp.float32)
    terms = jnp.concatenate([high, part - high], axis=1).astype(jnp.bfloat16)
    for head in range(KEY_VALUE_HEADS):
        for t in range(DECODE_STEPS):
            ready[head, positions + t // 2, t % 2, :] = terms[t]
    rows = pl.ds(positions, DECODE_STEPS // 2)
    stores.append(
        pltpu.make_async_copy(ready.at[:, rows], out.at[:, rows], sems.at[2 + 2 * SPLITS])
    )
    stores[-1].start()
    for store in stores:
        store.wait()


def attend_kernel(
    info, lows, up0, up1, up2, up3, turn, cached, newest, out, query
):
    ups = (up0, up1, up2, up3)
    length = info[0]
    place = info[1]
    low = jnp.sum(lows[...], axis=0)
    rank = low.shape[1]
    high = low.astype(jnp.bfloat16).astype(jnp.float32)
    rest = low - high
    middle = rest.astype(jnp.bfloat16).astype(jnp.float32)
    terms = jnp.concatenate([high, middle, rest - middle, jnp.zeros_like(low)], axis=0).astype(
        jnp.bfloat16
    )
    cosine = turn[0]
    sine = turn[1]
    for j in range(BLOCK):
        start = (j % BLOCK_CORE) * (up0.shape[0] // BLOCK_CORE)
        both = ups[j // BLOCK_CORE]
        extra = jnp.dot(
            terms, both[start : start + rank, :], preferred_element_type=jnp.float32
        )
        base = both[start + rank : start + rank + 16, :].astype(jnp.float32)
        raw = ((base[8:12] + base[4:8]) + base[0:4]) + ((extra[8:12] + extra[4:8]) + extra[0:4])
        for i in range(2):
            head = raw[:, i * HEAD_WIDTH : (i + 1) * HEAD_WIDTH]
            row = (2 * j + i) * DECODE_STEPS
            query[row : row + DECODE_STEPS, :] = head * cosine + pltpu.roll(head, 64, 1) * sine
    queries = query[...].astype(jnp.bfloat16)
    scale = 1.0 / math.sqrt(HEAD_WIDTH)
    own = pl.ds(pl.multiple_of(info[2] * HEAD_WIDTH, HEAD_WIDTH), HEAD_WIDTH)
    token = newest[:, 0, 0, own].astype(jnp.float32)
    token = token * cosine + pltpu.roll(token, 64, 1) * sine
    blank = jnp.zeros((HEAD_WIDTH - DECODE_STEPS, HEAD_WIDTH), jnp.float32)
    fresh_key = jnp.concatenate([token, blank], axis=0).astype(jnp.bfloat16)
    fresh_value = jnp.concatenate(
        [newest[:, 0, 1, own].astype(jnp.float32), blank], axis=0
    ).astype(jnp.bfloat16)
    n_src = cached.shape[0]
    pairs = cached.shape[1] - DECODE_STEPS
    column = lax.broadcasted_iota(jnp.int32, (ROWS, pairs), 1)
    row = lax.broadcasted_iota(jnp.int32, (ROWS, HEAD_WIDTH), 0)
    lane = lax.broadcasted_iota(jnp.int32, (ROWS, HEAD_WIDTH), 1)
    keyed = lax.rem(column, 2) == 0
    position = lax.div(column, 2)
    contract = (((1,), (1,)), ((), ()))
    masks = []
    scores = []
    for j in range(n_src):
        s = lax.dot_general(queries, cached[j, :pairs, :], contract, preferred_element_type=jnp.float32)
        start = (j * BLOCK + place) * (pairs // 2)
        ok = keyed & (position + start < length)
        masks.append(ok)
        scores.append(jnp.where(ok, s * scale, MASKED))
    s = lax.dot_general(queries, fresh_key, contract, preferred_element_type=jnp.float32)
    ok = (lane <= lax.rem(row, DECODE_STEPS)) & (place == 0)
    masks.append(ok)
    scores.append(jnp.where(ok, s * scale, MASKED))
    top = jnp.max(scores[-1], axis=-1, keepdims=True)
    for s in scores[:-1]:
        top = jnp.maximum(top, jnp.max(s, axis=-1, keepdims=True))
    total = jnp.zeros_like(top)
    summed = jnp.zeros((ROWS, HEAD_WIDTH), jnp.float32)
    for j in range(n_src + 1):
        weight = jnp.where(masks[j], jnp.exp(scores[j] - top), 0.0)
        total = total + jnp.sum(weight, axis=-1, keepdims=True)
        if j < n_src:
            weight, values = pltpu.roll(weight, 1, 1), cached[j, :pairs, :]
        else:
            values = fresh_value
        summed = summed + jnp.dot(
            weight.astype(jnp.bfloat16), values, preferred_element_type=jnp.float32
        )
    stats = jnp.where(lane < 64, top, total)
    each = 2 * DECODE_STEPS
    for d in range(BLOCK):
        out[place ^ d, :each, :] = summed[d * each : (d + 1) * each, :]
        out[place ^ d, each:, :] = stats[d * each : (d + 1) * each, :]


def combine(parts):
    each = 2 * DECODE_STEPS
    summed, stats = parts[:, :each], parts[:, each:]
    tops, totals = stats[:, :, :1], stats[:, :, 64:65]
    factor = jnp.exp(tops - jnp.max(tops, axis=0, keepdims=True))
    whole = jnp.sum(summed * factor, axis=0) / jnp.sum(totals * factor, axis=0)
    whole = whole.reshape(2, DECODE_STEPS, HEAD_WIDTH).swapaxes(0, 1)
    return whole.reshape(DECODE_STEPS, 2 * HEAD_WIDTH).astype(jnp.bfloat16)


def local(hidden, current_weight, down_factors, up_factors, cache, step_key_value, lengths):
    plane = ("y", "x", "core")
    block = ("x", "core")
    shard = lax.axis_index(plane)
    place = lax.axis_index(block)
    key_head = lax.axis_index(("role", "y"))
    rows = hidden.reshape(DECODE_STEPS, -1)
    down = down_factors[0, 0].T
    vmem = pl.BlockSpec(memory_space=pltpu.VMEM)
    smem = pl.BlockSpec(memory_space=pltpu.SMEM)
    hbm = pl.BlockSpec(memory_space=pl.ANY)
    positions = cache.shape[1]
    sent = jax.ShapeDtypeStruct(
        (KEY_VALUE_HEADS, positions + DECODE_STEPS // 2, 2, HEAD_WIDTH), cache.dtype
    )
    sent = pl.pallas_call(
        split_kernel,
        out_shape=sent,
        in_specs=[smem] + [hbm] * 3,
        out_specs=hbm,
        scratch_shapes=[
            pltpu.VMEM((rows.shape[0], down.shape[1]), rows.dtype),
            pltpu.VMEM(down.shape, down.dtype),
            pltpu.VMEM(cache.shape[1:], cache.dtype),
            pltpu.VMEM(sent.shape, sent.dtype),
            pltpu.SemaphoreType.DMA((3 + 2 * SPLITS,)),
        ],
        compiler_params=pltpu.CompilerParams(vmem_limit_bytes=58 * 2**20),
        name="split",
    )(shard[None].astype(jnp.int32), rows, down, cache[0])
    cached = lax.all_to_all(sent, ("role", "y"), 0, 0)
    rank = down.shape[0]
    terms = cached[:, positions:].astype(jnp.float32).reshape(2, -1, DECODE_STEPS, 2, rank)
    terms = jnp.sum(terms[:, :, :, 1] + terms[:, :, :, 0], axis=1)
    low = jnp.concatenate([terms[0], -terms[1]], axis=1)
    lows = lax.all_to_all(jnp.broadcast_to(low, (BLOCK,) + low.shape), block, 0, 0)
    cached = cached.reshape(KEY_VALUE_HEADS, -1, HEAD_WIDTH)

    base = jnp.dot(rows, current_weight, preferred_element_type=jnp.float32)
    high = lax.reduce_precision(base, 8, 7)
    middle = lax.reduce_precision(base - high, 8, 7)
    parts = [high, middle, base - high - middle, jnp.zeros_like(base)]
    parts = [term.astype(jnp.bfloat16) for term in parts]
    up = jnp.concatenate([up_factors.reshape(-1, up_factors.shape[-1])] + parts, axis=0)
    up = jnp.concatenate([up, swapped(up, "core", 1)], axis=0)
    ups = [up] + [swapped(up, "x", m) for m in range(1, BLOCK_X)]

    steps_pos = lengths[None, :] + jnp.arange(DECODE_STEPS, dtype=jnp.int32)[:, None]
    cosine, sine = angles(steps_pos[:, 0])
    turn = jnp.stack(
        [
            jnp.concatenate([cosine, cosine], axis=-1),
            jnp.concatenate([-sine, sine], axis=-1),
        ]
    )
    info = jnp.stack([lengths[0], place, key_head]).astype(jnp.int32)

    parts = pl.pallas_call(
        attend_kernel,
        out_shape=jax.ShapeDtypeStruct((BLOCK, 4 * DECODE_STEPS, HEAD_WIDTH), jnp.float32),
        in_specs=[smem] + [vmem] * 8,
        out_specs=vmem,
        scratch_shapes=[pltpu.VMEM((ROWS, HEAD_WIDTH), jnp.float32)],
        compiler_params=pltpu.CompilerParams(vmem_limit_bytes=16 * 2**20),
        name="attend",
    )(info, lows, *ups, turn, cached, step_key_value)
    parts = lax.all_to_all(parts, block, 0, 0)
    out = combine(parts)
    return out[:, None, :]


def solution(mesh):
    role, grp, tp = mesh.devices.shape
    finer = Mesh(
        mesh.devices.reshape(role, grp, tp // BLOCK, BLOCK_X, BLOCK_CORE),
        ("role", "grp", "y", "x", "core"),
    )
    tp = ("y", "x", "core")
    both = ("role",) + tp
    placed = (
        P(None, "grp", None),
        P(None, both),
        P("role", "grp", tp, None),
        P(None, "grp", None, both),
        P("grp", both, None, None),
        P(None, "grp", None, None),
        P("grp"),
    )
    return jax.shard_map(
        local, mesh=finer, in_specs=placed, out_specs=P(None, "grp", both), check_vma=False
    )
```

```python
import math

import jax
import jax.numpy as jnp
from jax import lax
from jax.experimental import pallas as pl
from jax.experimental.pallas import tpu as pltpu
from jax.sharding import Mesh, PartitionSpec as P

QUERY_HEADS = 128
KEY_VALUE_HEADS = 8
HEAD_WIDTH = 128
DECODE_STEPS = 4
BLOCK_X = 4
BLOCK_CORE = 2
BLOCK = BLOCK_X * BLOCK_CORE
SHARE = QUERY_HEADS // KEY_VALUE_HEADS
ROWS = SHARE * DECODE_STEPS
MASKED = -1e30


def angles(pos):
    half = HEAD_WIDTH // 2
    freq = jnp.exp(
        jnp.arange(half, dtype=jnp.float32) * (-2.0 * math.log(500000.0) / HEAD_WIDTH)
    )
    angle = pos.astype(jnp.float32)[:, None] * freq
    return jnp.cos(angle), jnp.sin(angle)


def swapped(block, axis, apart):
    count = lax.axis_size(axis)
    return lax.ppermute(block, axis, [(i, i ^ apart) for i in range(count)])


SPLITS = 4


def split_kernel(info, hidden, down, cache, out, some, factor, held, ready, sems):
    positions = cache.shape[0]
    piece = positions // SPLITS
    depth = down.shape[1]
    own = pl.ds(pl.multiple_of(info[0] * depth, depth), depth)
    fetches = [
        pltpu.make_async_copy(hidden.at[:, own], some, sems.at[0]),
        pltpu.make_async_copy(down, factor, sems.at[1]),
    ]
    for k in range(SPLITS):
        rows = pl.ds(k * piece, piece)
        fetches.append(pltpu.make_async_copy(cache.at[rows], held.at[rows], sems.at[2 + k]))
    for fetch in fetches:
        fetch.start()
    stores = []
    for k in range(SPLITS):
        fetches[2 + k].wait()
        rows = slice(k * piece, (k + 1) * piece)
        for head in range(KEY_VALUE_HEADS):
            columns = slice(head * HEAD_WIDTH, (head + 1) * HEAD_WIDTH)
            ready[head, rows] = held[rows, :, columns]
        rows = pl.ds(k * piece, piece)
        stores.append(
            pltpu.make_async_copy(ready.at[:, rows], out.at[:, rows], sems.at[2 + SPLITS + k])
        )
        stores[-1].start()
    fetches[0].wait()
    fetches[1].wait()
    part = lax.dot_general(
        some[...], factor[...], (((1,), (1,)), ((), ())), preferred_element_type=jnp.float32
    )
    high = part.astype(jnp.bfloat16).astype(jnp.float32)
    terms = jnp.concatenate([high, part - high], axis=1).astype(jnp.bfloat16)
    for head in range(KEY_VALUE_HEADS):
        for t in range(DECODE_STEPS):
            ready[head, positions + t // 2, t % 2, :] = terms[t]
    rows = pl.ds(positions, DECODE_STEPS // 2)
    stores.append(
        pltpu.make_async_copy(ready.at[:, rows], out.at[:, rows], sems.at[2 + 2 * SPLITS])
    )
    stores[-1].start()
    for store in stores:
        store.wait()


def attend_kernel(
    info, lows, up0, up1, up2, up3, turn, cached, newest, out, query
):
    ups = (up0, up1, up2, up3)
    length = info[0]
    place = info[1]
    low = jnp.sum(lows[...], axis=0)
    rank = low.shape[1]
    high = low.astype(jnp.bfloat16).astype(jnp.float32)
    rest = low - high
    middle = rest.astype(jnp.bfloat16).astype(jnp.float32)
    terms = jnp.concatenate([high, middle, rest - middle, jnp.zeros_like(low)], axis=0).astype(
        jnp.bfloat16
    )
    cosine = turn[0]
    sine = turn[1]
    for j in range(BLOCK):
        start = (j % BLOCK_CORE) * (up0.shape[0] // BLOCK_CORE)
        both = ups[j // BLOCK_CORE]
        extra = jnp.dot(
            terms, both[start : start + rank, :], preferred_element_type=jnp.float32
        )
        base = both[start + rank : start + rank + 16, :].astype(jnp.float32)
        raw = ((base[8:12] + base[4:8]) + base[0:4]) + ((extra[8:12] + extra[4:8]) + extra[0:4])
        for i in range(2):
            head = raw[:, i * HEAD_WIDTH : (i + 1) * HEAD_WIDTH]
            row = (2 * j + i) * DECODE_STEPS
            query[row : row + DECODE_STEPS, :] = head * cosine + pltpu.roll(head, 64, 1) * sine
    queries = query[...].astype(jnp.bfloat16)
    scale = 1.0 / math.sqrt(HEAD_WIDTH)
    own = pl.ds(pl.multiple_of(info[2] * HEAD_WIDTH, HEAD_WIDTH), HEAD_WIDTH)
    token = newest[:, 0, 0, own].astype(jnp.float32)
    token = token * cosine + pltpu.roll(token, 64, 1) * sine
    blank = jnp.zeros((HEAD_WIDTH - DECODE_STEPS, HEAD_WIDTH), jnp.float32)
    fresh_key = jnp.concatenate([token, blank], axis=0).astype(jnp.bfloat16)
    fresh_value = jnp.concatenate(
        [newest[:, 0, 1, own].astype(jnp.float32), blank], axis=0
    ).astype(jnp.bfloat16)
    n_src = cached.shape[0]
    pairs = cached.shape[1] - DECODE_STEPS
    column = lax.broadcasted_iota(jnp.int32, (ROWS, pairs), 1)
    row = lax.broadcasted_iota(jnp.int32, (ROWS, HEAD_WIDTH), 0)
    lane = lax.broadcasted_iota(jnp.int32, (ROWS, HEAD_WIDTH), 1)
    keyed = lax.rem(column, 2) == 0
    position = lax.div(column, 2)
    contract = (((1,), (1,)), ((), ()))
    masks = []
    scores = []
    for j in range(n_src):
        s = lax.dot_general(queries, cached[j, :pairs, :], contract, preferred_element_type=jnp.float32)
        start = (j * BLOCK + place) * (pairs // 2)
        ok = keyed & (position + start < length)
        masks.append(ok)
        scores.append(jnp.where(ok, s * scale, MASKED))
    s = lax.dot_general(queries, fresh_key, contract, preferred_element_type=jnp.float32)
    ok = (lane <= lax.rem(row, DECODE_STEPS)) & (place == 0)
    masks.append(ok)
    scores.append(jnp.where(ok, s * scale, MASKED))
    top = jnp.max(scores[-1], axis=-1, keepdims=True)
    for s in scores[:-1]:
        top = jnp.maximum(top, jnp.max(s, axis=-1, keepdims=True))
    total = jnp.zeros_like(top)
    summed = jnp.zeros((ROWS, HEAD_WIDTH), jnp.float32)
    for j in range(n_src + 1):
        weight = jnp.where(masks[j], jnp.exp(scores[j] - top), 0.0)
        total = total + jnp.sum(weight, axis=-1, keepdims=True)
        if j < n_src:
            weight, values = pltpu.roll(weight, 1, 1), cached[j, :pairs, :]
        else:
            values = fresh_value
        summed = summed + jnp.dot(
            weight.astype(jnp.bfloat16), values, preferred_element_type=jnp.float32
        )
    top = jnp.broadcast_to(top, summed.shape)
    total = jnp.broadcast_to(total, summed.shape)
    each = 2 * DECODE_STEPS
    for d in range(BLOCK):
        rows = slice(d * each, (d + 1) * each)
        for i, value in enumerate((summed, top, total)):
            out[place ^ d, i * each : (i + 1) * each, :] = value[rows, :]


def combine(parts):
    each = 2 * DECODE_STEPS
    summed, tops, totals = (
        [parts[d, i * each : (i + 1) * each] for d in range(BLOCK)] for i in range(3)
    )
    top = tops[0]
    for other in tops[1:]:
        top = jnp.maximum(top, other)
    above, below = 0.0, 0.0
    for d in range(BLOCK):
        factor = jnp.exp(tops[d] - top)
        above = above + summed[d] * factor
        below = below + totals[d] * factor
    whole = (above / below).astype(jnp.bfloat16)
    return jnp.concatenate([whole[:DECODE_STEPS], whole[DECODE_STEPS:]], axis=1)


def local(hidden, current_weight, down_factors, up_factors, cache, step_key_value, lengths):
    plane = ("y", "x", "core")
    block = ("x", "core")
    shard = lax.axis_index(plane)
    place = lax.axis_index(block)
    key_head = lax.axis_index(("role", "y"))
    rows = hidden.reshape(DECODE_STEPS, -1)
    down = down_factors[0, 0].T
    vmem = pl.BlockSpec(memory_space=pltpu.VMEM)
    smem = pl.BlockSpec(memory_space=pltpu.SMEM)
    hbm = pl.BlockSpec(memory_space=pl.ANY)
    positions = cache.shape[1]
    sent = jax.ShapeDtypeStruct(
        (KEY_VALUE_HEADS, positions + DECODE_STEPS // 2, 2, HEAD_WIDTH), cache.dtype
    )
    sent = pl.pallas_call(
        split_kernel,
        out_shape=sent,
        in_specs=[smem] + [hbm] * 3,
        out_specs=hbm,
        scratch_shapes=[
            pltpu.VMEM((rows.shape[0], down.shape[1]), rows.dtype),
            pltpu.VMEM(down.shape, down.dtype),
            pltpu.VMEM(cache.shape[1:], cache.dtype),
            pltpu.VMEM(sent.shape, sent.dtype),
            pltpu.SemaphoreType.DMA((3 + 2 * SPLITS,)),
        ],
        compiler_params=pltpu.CompilerParams(vmem_limit_bytes=58 * 2**20),
        name="split",
    )(shard[None].astype(jnp.int32), rows, down, cache[0])
    cached = lax.all_to_all(sent, ("role", "y"), 0, 0)
    rank = down.shape[0]
    terms = cached[:, positions:].astype(jnp.float32).reshape(2, -1, DECODE_STEPS, 2, rank)
    terms = jnp.sum(terms[:, :, :, 1] + terms[:, :, :, 0], axis=1)
    low = jnp.concatenate([terms[0], -terms[1]], axis=1)
    lows = lax.all_to_all(jnp.broadcast_to(low, (BLOCK,) + low.shape), block, 0, 0)
    cached = cached.reshape(KEY_VALUE_HEADS, -1, HEAD_WIDTH)

    base = jnp.dot(rows, current_weight, preferred_element_type=jnp.float32)
    high = lax.reduce_precision(base, 8, 7)
    middle = lax.reduce_precision(base - high, 8, 7)
    parts = [high, middle, base - high - middle, jnp.zeros_like(base)]
    parts = [term.astype(jnp.bfloat16) for term in parts]
    up = jnp.concatenate([up_factors.reshape(-1, up_factors.shape[-1])] + parts, axis=0)
    up = jnp.concatenate([up, swapped(up, "core", 1)], axis=0)
    ups = [up] + [swapped(up, "x", m) for m in range(1, BLOCK_X)]

    steps_pos = lengths[None, :] + jnp.arange(DECODE_STEPS, dtype=jnp.int32)[:, None]
    cosine, sine = angles(steps_pos[:, 0])
    turn = jnp.stack(
        [
            jnp.concatenate([cosine, cosine], axis=-1),
            jnp.concatenate([-sine, sine], axis=-1),
        ]
    )
    info = jnp.stack([lengths[0], place, key_head]).astype(jnp.int32)

    parts = pl.pallas_call(
        attend_kernel,
        out_shape=jax.ShapeDtypeStruct((BLOCK, 6 * DECODE_STEPS, HEAD_WIDTH), jnp.float32),
        in_specs=[smem] + [vmem] * 8,
        out_specs=vmem,
        scratch_shapes=[pltpu.VMEM((ROWS, HEAD_WIDTH), jnp.float32)],
        compiler_params=pltpu.CompilerParams(vmem_limit_bytes=16 * 2**20),
        name="attend",
    )(info, lows, *ups, turn, cached, step_key_value)
    parts = lax.all_to_all(parts, block, 0, 0)
    out = combine(parts)
    return out[:, None, :]


def solution(mesh):
    role, grp, tp = mesh.devices.shape
    finer = Mesh(
        mesh.devices.reshape(role, grp, tp // BLOCK, BLOCK_X, BLOCK_CORE),
        ("role", "grp", "y", "x", "core"),
    )
    tp = ("y", "x", "core")
    both = ("role",) + tp
    placed = (
        P(None, "grp", None),
        P(None, both),
        P("role", "grp", tp, None),
        P(None, "grp", None, both),
        P("grp", both, None, None),
        P(None, "grp", None, None),
        P("grp"),
    )
    return jax.shard_map(
        local, mesh=finer, in_specs=placed, out_specs=P(None, "grp", both), check_vma=False
    )
```

```python
import math

import jax
import jax.numpy as jnp
from jax import lax
from jax.experimental import pallas as pl
from jax.experimental.pallas import tpu as pltpu
from jax.sharding import Mesh, PartitionSpec as P

QUERY_HEADS = 128
KEY_VALUE_HEADS = 8
HEAD_WIDTH = 128
DECODE_STEPS = 4
BLOCK_X = 4
BLOCK_CORE = 2
BLOCK = BLOCK_X * BLOCK_CORE
SHARE = QUERY_HEADS // KEY_VALUE_HEADS
ROWS = SHARE * DECODE_STEPS
MASKED = -1e30


def angles(pos):
    half = HEAD_WIDTH // 2
    freq = jnp.exp(
        jnp.arange(half, dtype=jnp.float32) * (-2.0 * math.log(500000.0) / HEAD_WIDTH)
    )
    angle = pos.astype(jnp.float32)[:, None] * freq
    return jnp.cos(angle), jnp.sin(angle)


def swapped(block, axis, apart):
    count = lax.axis_size(axis)
    return lax.ppermute(block, axis, [(i, i ^ apart) for i in range(count)])


def split_kernel(info, hidden, down, cache, out):
    depth = down.shape[1]
    own = pl.ds(pl.multiple_of(info[0] * depth, depth), depth)
    part = lax.dot_general(
        hidden[:, own], down[...], (((1,), (1,)), ((), ())), preferred_element_type=jnp.float32
    )
    high = part.astype(jnp.bfloat16).astype(jnp.float32)
    terms = jnp.concatenate([high, part - high], axis=1).astype(jnp.bfloat16)
    share = cache.shape[0] // BLOCK
    for head in range(KEY_VALUE_HEADS):
        columns = slice(head * HEAD_WIDTH, (head + 1) * HEAD_WIDTH)
        for d in range(BLOCK):
            to = head * BLOCK + d
            out[to, :share] = cache[d * share : (d + 1) * share, :, columns]
            for t in range(DECODE_STEPS):
                out[to, share + t // 2, t % 2, :] = terms[t]


def attend_kernel(
    info, pos, pick, up0, up1, up2, up3, turn, cached, newest, out, query
):
    ups = (up0, up1, up2, up3)
    length = info[0]
    place = info[1]
    sums = jnp.dot(pick[...], cached[...], preferred_element_type=jnp.float32)
    half = HEAD_WIDTH // 2
    low = [
        sums[i * DECODE_STEPS : (i + 1) * DECODE_STEPS, :half]
        + sums[i * DECODE_STEPS : (i + 1) * DECODE_STEPS, half:]
        for i in range(2)
    ]
    low = jnp.concatenate(low, axis=1)
    rank = low.shape[1]
    high = low.astype(jnp.bfloat16).astype(jnp.float32)
    rest = low - high
    middle = rest.astype(jnp.bfloat16).astype(jnp.float32)
    terms = jnp.concatenate([high, middle, rest - middle, jnp.zeros_like(low)], axis=0).astype(
        jnp.bfloat16
    )
    cosine = turn[0]
    sine = turn[1]
    for j in range(BLOCK):
        step = up0.shape[0] // BLOCK_CORE
        start = pl.multiple_of((place ^ j) % BLOCK_CORE * step, 16)
        both = ups[j // BLOCK_CORE]
        extra = jnp.dot(
            terms, both[pl.ds(start, rank), :], preferred_element_type=jnp.float32
        )
        base = both[pl.ds(start + rank, 16), :].astype(jnp.float32)
        raw = ((base[8:12] + base[4:8]) + base[0:4]) + ((extra[8:12] + extra[4:8]) + extra[0:4])
        for i in range(2):
            head = raw[:, i * HEAD_WIDTH : (i + 1) * HEAD_WIDTH]
            row = (2 * j + i) * DECODE_STEPS
            query[row : row + DECODE_STEPS, :] = head * cosine + pltpu.roll(head, 64, 1) * sine
    queries = query[...].astype(jnp.bfloat16)
    scale = 1.0 / math.sqrt(HEAD_WIDTH)
    own = pl.ds(pl.multiple_of(info[2] * HEAD_WIDTH, HEAD_WIDTH), HEAD_WIDTH)
    token = newest[:, 0, 0, own].astype(jnp.float32)
    token = token * cosine + pltpu.roll(token, 64, 1) * sine
    blank = jnp.zeros((HEAD_WIDTH - DECODE_STEPS, HEAD_WIDTH), jnp.float32)
    fresh_key = jnp.concatenate([token, blank], axis=0).astype(jnp.bfloat16)
    fresh_value = jnp.concatenate(
        [newest[:, 0, 1, own].astype(jnp.float32), blank], axis=0
    ).astype(jnp.bfloat16)
    chunk = 256
    n_src = cached.shape[0] // chunk
    blocks = [slice(j * chunk, (j + 1) * chunk) for j in range(n_src)]
    row = lax.broadcasted_iota(jnp.int32, (ROWS, HEAD_WIDTH), 0)
    lane = lax.broadcasted_iota(jnp.int32, (ROWS, HEAD_WIDTH), 1)
    contract = (((1,), (1,)), ((), ()))
    masks = []
    scores = []
    for j in range(n_src):
        keys = cached[blocks[j], :]
        s = lax.dot_general(queries, keys, contract, preferred_element_type=jnp.float32)
        ok = jnp.broadcast_to(pos[:, blocks[j]] < length, s.shape)
        masks.append(ok)
        scores.append(jnp.where(ok, s * scale, MASKED))
    s = lax.dot_general(queries, fresh_key, contract, preferred_element_type=jnp.float32)
    ok = (lane <= lax.rem(row, DECODE_STEPS)) & (place == 0)
    masks.append(ok)
    scores.append(jnp.where(ok, s * scale, MASKED))
    top = jnp.max(scores[-1], axis=-1, keepdims=True)
    for s in scores[:-1]:
        top = jnp.maximum(top, jnp.max(s, axis=-1, keepdims=True))
    total = jnp.zeros_like(top)
    summed = jnp.zeros((ROWS, HEAD_WIDTH), jnp.float32)
    for j in range(n_src + 1):
        weight = jnp.where(masks[j], jnp.exp(scores[j] - top), 0.0)
        total = total + jnp.sum(weight, axis=-1, keepdims=True)
        if j < n_src:
            weight, values = pltpu.roll(weight, 1, 1), cached[blocks[j], :]
        else:
            values = fresh_value
        summed = summed + jnp.dot(
            weight.astype(jnp.bfloat16), values, preferred_element_type=jnp.float32
        )
    top = jnp.broadcast_to(top, summed.shape)
    total = jnp.broadcast_to(total, summed.shape)
    each = 2 * DECODE_STEPS
    for d in range(BLOCK):
        rows = slice(d * each, (d + 1) * each)
        for i, value in enumerate((summed, top, total)):
            out[place ^ d, i * each : (i + 1) * each, :] = value[rows, :]


def combine(parts):
    each = 2 * DECODE_STEPS
    summed, tops, totals = (
        [parts[d, i * each : (i + 1) * each] for d in range(BLOCK)] for i in range(3)
    )
    top = tops[0]
    for other in tops[1:]:
        top = jnp.maximum(top, other)
    above, below = 0.0, 0.0
    for d in range(BLOCK):
        factor = jnp.exp(tops[d] - top)
        above = above + summed[d] * factor
        below = below + totals[d] * factor
    whole = (above / below).astype(jnp.bfloat16)
    return jnp.concatenate([whole[:DECODE_STEPS], whole[DECODE_STEPS:]], axis=1)


def local(hidden, current_weight, down_factors, up_factors, cache, step_key_value, lengths):
    plane = ("y", "x", "core")
    block = ("x", "core")
    shard = lax.axis_index(plane)
    place = lax.axis_index(block)
    key_head = lax.axis_index(("role", "y"))
    rows = hidden.reshape(DECODE_STEPS, -1)
    down = down_factors[0, 0].T
    vmem = pl.BlockSpec(memory_space=pltpu.VMEM)
    smem = pl.BlockSpec(memory_space=pltpu.SMEM)
    everyone = ("role",) + plane
    share = cache.shape[1] // BLOCK
    sent = pl.pallas_call(
        split_kernel,
        out_shape=jax.ShapeDtypeStruct(
            (lax.axis_size(everyone), share + DECODE_STEPS // 2, 2, HEAD_WIDTH), cache.dtype
        ),
        in_specs=[smem] + [vmem] * 3,
        out_specs=vmem,
        name="split",
    )(shard[None].astype(jnp.int32), rows, down, cache[0])
    cached = lax.all_to_all(sent, everyone, 0, 0)
    rows_each = 2 * cached.shape[1]
    cached = cached.reshape(-1, HEAD_WIDTH)
    column = jnp.arange(cached.shape[0], dtype=jnp.int32)
    source, inner = column // rows_each, column % rows_each
    pos = source * cache.shape[1] + place * share + inner // 2
    pos = jnp.where((inner < 2 * share) & (inner % 2 == 0), pos, jnp.int32(2**30))[None]
    step = jnp.arange(16, dtype=jnp.int32)[:, None]
    new = source < lax.axis_size(everyone) // 2
    wanted = (inner >= 2 * share) & (inner - 2 * share == step % DECODE_STEPS)
    wanted = wanted & (step // DECODE_STEPS == jnp.where(new, 0, 1))
    pick = jnp.where(wanted, jnp.where(new, 1.0, -1.0), 0.0).astype(jnp.bfloat16)

    rows, sent = lax.optimization_barrier((rows, sent))
    base = jnp.dot(rows, current_weight, preferred_element_type=jnp.float32)
    high = lax.reduce_precision(base, 8, 7)
    middle = lax.reduce_precision(base - high, 8, 7)
    parts = [high, middle, base - high - middle, jnp.zeros_like(base)]
    parts = [term.astype(jnp.bfloat16) for term in parts]
    up = jnp.concatenate([up_factors.reshape(-1, up_factors.shape[-1])] + parts, axis=0)
    up = lax.all_gather(up, "core", axis=0, tiled=True)
    ups = [up] + [swapped(up, "x", m) for m in range(1, BLOCK_X)]

    steps_pos = lengths[None, :] + jnp.arange(DECODE_STEPS, dtype=jnp.int32)[:, None]
    cosine, sine = angles(steps_pos[:, 0])
    turn = jnp.stack(
        [
            jnp.concatenate([cosine, cosine], axis=-1),
            jnp.concatenate([-sine, sine], axis=-1),
        ]
    )
    info = jnp.stack([lengths[0], place, key_head]).astype(jnp.int32)

    parts = pl.pallas_call(
        attend_kernel,
        out_shape=jax.ShapeDtypeStruct((BLOCK, 6 * DECODE_STEPS, HEAD_WIDTH), jnp.float32),
        in_specs=[smem] + [vmem] * 9,
        out_specs=vmem,
        scratch_shapes=[pltpu.VMEM((ROWS, HEAD_WIDTH), jnp.float32)],
        compiler_params=pltpu.CompilerParams(vmem_limit_bytes=16 * 2**20),
        name="attend",
    )(info, pos, pick, *ups, turn, cached, step_key_value)
    parts = lax.all_to_all(parts, block, 0, 0)
    out = combine(parts)
    return out[:, None, :]


def solution(mesh):
    role, grp, tp = mesh.devices.shape
    finer = Mesh(
        mesh.devices.reshape(role, grp, tp // BLOCK, BLOCK_X, BLOCK_CORE),
        ("role", "grp", "y", "x", "core"),
    )
    tp = ("y", "x", "core")
    both = ("role",) + tp
    placed = (
        P(None, "grp", None),
        P(None, both),
        P("role", "grp", tp, None),
        P(None, "grp", None, both),
        P("grp", both, None, None),
        P(None, "grp", None, None),
        P("grp"),
    )
    return jax.shard_map(
        local, mesh=finer, in_specs=placed, out_specs=P(None, "grp", both), check_vma=False
    )
```

```python
import math

import jax
import jax.numpy as jnp
from jax import lax
from jax.experimental import pallas as pl
from jax.experimental.pallas import tpu as pltpu
from jax.sharding import Mesh, PartitionSpec as P

QUERY_HEADS = 128
KEY_VALUE_HEADS = 8
HEAD_WIDTH = 128
DECODE_STEPS = 4
BLOCK_X = 4
BLOCK_CORE = 2
BLOCK = BLOCK_X * BLOCK_CORE
SHARE = QUERY_HEADS // KEY_VALUE_HEADS
ROWS = SHARE * DECODE_STEPS
MASKED = -1e30


def angles(pos):
    half = HEAD_WIDTH // 2
    freq = jnp.exp(
        jnp.arange(half, dtype=jnp.float32) * (-2.0 * math.log(500000.0) / HEAD_WIDTH)
    )
    angle = pos.astype(jnp.float32)[:, None] * freq
    return jnp.cos(angle), jnp.sin(angle)


def swapped(block, axis, apart):
    count = lax.axis_size(axis)
    return lax.ppermute(block, axis, [(i, i ^ apart) for i in range(count)])


SPLITS = 4


def split_kernel(info, hidden, down, cache, out, some, factor, held, ready, sems):
    share = cache.shape[0] // BLOCK
    piece = cache.shape[0] // SPLITS
    depth = down.shape[1]
    own = pl.ds(pl.multiple_of(info[0] * depth, depth), depth)
    fetches = [
        pltpu.make_async_copy(hidden.at[:, own], some, sems.at[0]),
        pltpu.make_async_copy(down, factor, sems.at[1]),
    ]
    for k in range(SPLITS):
        rows = pl.ds(k * piece, piece)
        fetches.append(pltpu.make_async_copy(cache.at[rows], held.at[rows], sems.at[2 + k]))
    for fetch in fetches:
        fetch.start()
    fetches[0].wait()
    fetches[1].wait()
    part = lax.dot_general(
        some[...], factor[...], (((1,), (1,)), ((), ())), preferred_element_type=jnp.float32
    )
    high = part.astype(jnp.bfloat16).astype(jnp.float32)
    terms = jnp.concatenate([high, part - high], axis=1).astype(jnp.bfloat16)
    stores = []
    each = BLOCK // SPLITS
    for k in range(SPLITS):
        fetches[2 + k].wait()
        for d in range(k * each, (k + 1) * each):
            for head in range(KEY_VALUE_HEADS):
                columns = slice(head * HEAD_WIDTH, (head + 1) * HEAD_WIDTH)
                ready[head, d, :share] = held[d * share : (d + 1) * share, :, columns]
                for t in range(DECODE_STEPS):
                    ready[head, d, share + t // 2, t % 2, :] = terms[t]
        rows = pl.ds(k * each, each)
        stores.append(
            pltpu.make_async_copy(ready.at[:, rows], out.at[:, rows], sems.at[2 + SPLITS + k])
        )
        stores[-1].start()
    for store in stores:
        store.wait()


def attend_kernel(
    info, pos, pick, up0, up1, up2, up3, turn, cached, newest, out, query
):
    ups = (up0, up1, up2, up3)
    length = info[0]
    place = info[1]
    sums = jnp.dot(pick[...], cached[...], preferred_element_type=jnp.float32)
    half = HEAD_WIDTH // 2
    low = [
        sums[i * DECODE_STEPS : (i + 1) * DECODE_STEPS, :half]
        + sums[i * DECODE_STEPS : (i + 1) * DECODE_STEPS, half:]
        for i in range(2)
    ]
    low = jnp.concatenate(low, axis=1)
    rank = low.shape[1]
    high = low.astype(jnp.bfloat16).astype(jnp.float32)
    rest = low - high
    middle = rest.astype(jnp.bfloat16).astype(jnp.float32)
    terms = jnp.concatenate([high, middle, rest - middle, jnp.zeros_like(low)], axis=0).astype(
        jnp.bfloat16
    )
    cosine = turn[0]
    sine = turn[1]
    for j in range(BLOCK):
        step = up0.shape[0] // BLOCK_CORE
        start = pl.multiple_of((place ^ j) % BLOCK_CORE * step, 16)
        both = ups[j // BLOCK_CORE]
        extra = jnp.dot(
            terms, both[pl.ds(start, rank), :], preferred_element_type=jnp.float32
        )
        base = both[pl.ds(start + rank, 16), :].astype(jnp.float32)
        raw = ((base[8:12] + base[4:8]) + base[0:4]) + ((extra[8:12] + extra[4:8]) + extra[0:4])
        for i in range(2):
            head = raw[:, i * HEAD_WIDTH : (i + 1) * HEAD_WIDTH]
            row = (2 * j + i) * DECODE_STEPS
            query[row : row + DECODE_STEPS, :] = head * cosine + pltpu.roll(head, 64, 1) * sine
    queries = query[...].astype(jnp.bfloat16)
    scale = 1.0 / math.sqrt(HEAD_WIDTH)
    own = pl.ds(pl.multiple_of(info[2] * HEAD_WIDTH, HEAD_WIDTH), HEAD_WIDTH)
    token = newest[:, 0, 0, own].astype(jnp.float32)
    token = token * cosine + pltpu.roll(token, 64, 1) * sine
    blank = jnp.zeros((HEAD_WIDTH - DECODE_STEPS, HEAD_WIDTH), jnp.float32)
    fresh_key = jnp.concatenate([token, blank], axis=0).astype(jnp.bfloat16)
    fresh_value = jnp.concatenate(
        [newest[:, 0, 1, own].astype(jnp.float32), blank], axis=0
    ).astype(jnp.bfloat16)
    chunk = 256
    n_src = cached.shape[0] // chunk
    blocks = [slice(j * chunk, (j + 1) * chunk) for j in range(n_src)]
    row = lax.broadcasted_iota(jnp.int32, (ROWS, HEAD_WIDTH), 0)
    lane = lax.broadcasted_iota(jnp.int32, (ROWS, HEAD_WIDTH), 1)
    contract = (((1,), (1,)), ((), ()))
    masks = []
    scores = []
    for j in range(n_src):
        keys = cached[blocks[j], :]
        s = lax.dot_general(queries, keys, contract, preferred_element_type=jnp.float32)
        ok = jnp.broadcast_to(pos[:, blocks[j]] < length, s.shape)
        masks.append(ok)
        scores.append(jnp.where(ok, s * scale, MASKED))
    s = lax.dot_general(queries, fresh_key, contract, preferred_element_type=jnp.float32)
    ok = (lane <= lax.rem(row, DECODE_STEPS)) & (place == 0)
    masks.append(ok)
    scores.append(jnp.where(ok, s * scale, MASKED))
    top = jnp.max(scores[-1], axis=-1, keepdims=True)
    for s in scores[:-1]:
        top = jnp.maximum(top, jnp.max(s, axis=-1, keepdims=True))
    total = jnp.zeros_like(top)
    summed = jnp.zeros((ROWS, HEAD_WIDTH), jnp.float32)
    for j in range(n_src + 1):
        weight = jnp.where(masks[j], jnp.exp(scores[j] - top), 0.0)
        total = total + jnp.sum(weight, axis=-1, keepdims=True)
        if j < n_src:
            weight, values = pltpu.roll(weight, 1, 1), cached[blocks[j], :]
        else:
            values = fresh_value
        summed = summed + jnp.dot(
            weight.astype(jnp.bfloat16), values, preferred_element_type=jnp.float32
        )
    top = jnp.broadcast_to(top, summed.shape)
    total = jnp.broadcast_to(total, summed.shape)
    each = 2 * DECODE_STEPS
    for d in range(BLOCK):
        rows = slice(d * each, (d + 1) * each)
        for i, value in enumerate((summed, top, total)):
            out[place ^ d, i * each : (i + 1) * each, :] = value[rows, :]


def combine(parts):
    each = 2 * DECODE_STEPS
    summed, tops, totals = (
        [parts[d, i * each : (i + 1) * each] for d in range(BLOCK)] for i in range(3)
    )
    top = tops[0]
    for other in tops[1:]:
        top = jnp.maximum(top, other)
    above, below = 0.0, 0.0
    for d in range(BLOCK):
        factor = jnp.exp(tops[d] - top)
        above = above + summed[d] * factor
        below = below + totals[d] * factor
    whole = (above / below).astype(jnp.bfloat16)
    return jnp.concatenate([whole[:DECODE_STEPS], whole[DECODE_STEPS:]], axis=1)


def local(hidden, current_weight, down_factors, up_factors, cache, step_key_value, lengths):
    plane = ("y", "x", "core")
    block = ("x", "core")
    shard = lax.axis_index(plane)
    place = lax.axis_index(block)
    key_head = lax.axis_index(("role", "y"))
    rows = hidden.reshape(DECODE_STEPS, -1)
    down = down_factors[0, 0].T
    vmem = pl.BlockSpec(memory_space=pltpu.VMEM)
    smem = pl.BlockSpec(memory_space=pltpu.SMEM)
    everyone = ("role",) + plane
    share = cache.shape[1] // BLOCK
    sent = jax.ShapeDtypeStruct(
        (KEY_VALUE_HEADS, BLOCK, share + DECODE_STEPS // 2, 2, HEAD_WIDTH), cache.dtype
    )
    hbm = pl.BlockSpec(memory_space=pl.ANY)
    sent = pl.pallas_call(
        split_kernel,
        out_shape=sent,
        in_specs=[smem] + [hbm] * 3,
        out_specs=hbm,
        scratch_shapes=[
            pltpu.VMEM((rows.shape[0], down.shape[1]), rows.dtype),
            pltpu.VMEM(down.shape, down.dtype),
            pltpu.VMEM(cache.shape[1:], cache.dtype),
            pltpu.VMEM(sent.shape, sent.dtype),
            pltpu.SemaphoreType.DMA((2 + 2 * SPLITS,)),
        ],
        compiler_params=pltpu.CompilerParams(vmem_limit_bytes=58 * 2**20),
        name="split",
    )(shard[None].astype(jnp.int32), rows, down, cache[0])
    sent = sent.reshape((-1,) + sent.shape[2:])
    cached = lax.all_to_all(sent, everyone, 0, 0)
    rows_each = 2 * cached.shape[1]
    cached = cached.reshape(-1, HEAD_WIDTH)
    column = jnp.arange(cached.shape[0], dtype=jnp.int32)
    source, inner = column // rows_each, column % rows_each
    pos = source * cache.shape[1] + place * share + inner // 2
    pos = jnp.where((inner < 2 * share) & (inner % 2 == 0), pos, jnp.int32(2**30))[None]
    step = jnp.arange(16, dtype=jnp.int32)[:, None]
    new = source < lax.axis_size(everyone) // 2
    wanted = (inner >= 2 * share) & (inner - 2 * share == step % DECODE_STEPS)
    wanted = wanted & (step // DECODE_STEPS == jnp.where(new, 0, 1))
    pick = jnp.where(wanted, jnp.where(new, 1.0, -1.0), 0.0).astype(jnp.bfloat16)

    rows, sent = lax.optimization_barrier((rows, sent))
    base = jnp.dot(rows, current_weight, preferred_element_type=jnp.float32)
    high = lax.reduce_precision(base, 8, 7)
    middle = lax.reduce_precision(base - high, 8, 7)
    parts = [high, middle, base - high - middle, jnp.zeros_like(base)]
    parts = [term.astype(jnp.bfloat16) for term in parts]
    up = jnp.concatenate([up_factors.reshape(-1, up_factors.shape[-1])] + parts, axis=0)
    up = lax.all_gather(up, "core", axis=0, tiled=True)
    ups = [up] + [swapped(up, "x", m) for m in range(1, BLOCK_X)]

    steps_pos = lengths[None, :] + jnp.arange(DECODE_STEPS, dtype=jnp.int32)[:, None]
    cosine, sine = angles(steps_pos[:, 0])
    turn = jnp.stack(
        [
            jnp.concatenate([cosine, cosine], axis=-1),
            jnp.concatenate([-sine, sine], axis=-1),
        ]
    )
    info = jnp.stack([lengths[0], place, key_head]).astype(jnp.int32)

    parts = pl.pallas_call(
        attend_kernel,
        out_shape=jax.ShapeDtypeStruct((BLOCK, 6 * DECODE_STEPS, HEAD_WIDTH), jnp.float32),
        in_specs=[smem] + [vmem] * 9,
        out_specs=vmem,
        scratch_shapes=[pltpu.VMEM((ROWS, HEAD_WIDTH), jnp.float32)],
        compiler_params=pltpu.CompilerParams(vmem_limit_bytes=16 * 2**20),
        name="attend",
    )(info, pos, pick, *ups, turn, cached, step_key_value)
    parts = lax.all_to_all(parts, block, 0, 0)
    out = combine(parts)
    return out[:, None, :]


def solution(mesh):
    role, grp, tp = mesh.devices.shape
    finer = Mesh(
        mesh.devices.reshape(role, grp, tp // BLOCK, BLOCK_X, BLOCK_CORE),
        ("role", "grp", "y", "x", "core"),
    )
    tp = ("y", "x", "core")
    both = ("role",) + tp
    placed = (
        P(None, "grp", None),
        P(None, both),
        P("role", "grp", tp, None),
        P(None, "grp", None, both),
        P("grp", both, None, None),
        P(None, "grp", None, None),
        P("grp"),
    )
    return jax.shard_map(
        local, mesh=finer, in_specs=placed, out_specs=P(None, "grp", both), check_vma=False
    )
```

```python
import math

import jax
import jax.numpy as jnp
from jax import lax
from jax.experimental import pallas as pl
from jax.experimental.pallas import tpu as pltpu
from jax.sharding import Mesh, PartitionSpec as P

QUERY_HEADS = 128
KEY_VALUE_HEADS = 8
HEAD_WIDTH = 128
DECODE_STEPS = 4
BLOCK_X = 4
BLOCK_CORE = 2
BLOCK = BLOCK_X * BLOCK_CORE
SHARE = QUERY_HEADS // KEY_VALUE_HEADS
ROWS = SHARE * DECODE_STEPS
MASKED = -1e30


def angles(pos):
    half = HEAD_WIDTH // 2
    freq = jnp.exp(
        jnp.arange(half, dtype=jnp.float32) * (-2.0 * math.log(500000.0) / HEAD_WIDTH)
    )
    angle = pos.astype(jnp.float32)[:, None] * freq
    return jnp.cos(angle), jnp.sin(angle)


def swapped(block, axis, apart):
    count = lax.axis_size(axis)
    return lax.ppermute(block, axis, [(i, i ^ apart) for i in range(count)])


SPLITS = 4


def split_kernel(info, hidden, down, cache, out, some, factor, held, ready, sems):
    share = cache.shape[0] // BLOCK
    piece = cache.shape[0] // SPLITS
    depth = down.shape[1]
    own = pl.ds(pl.multiple_of(info[0] * depth, depth), depth)
    fetches = [
        pltpu.make_async_copy(hidden.at[:, own], some, sems.at[0]),
        pltpu.make_async_copy(down, factor, sems.at[1]),
    ]
    for k in range(SPLITS):
        rows = pl.ds(k * piece, piece)
        fetches.append(pltpu.make_async_copy(cache.at[rows], held.at[rows], sems.at[2 + k]))
    for fetch in fetches:
        fetch.start()
    fetches[0].wait()
    fetches[1].wait()
    part = lax.dot_general(
        some[...], factor[...], (((1,), (1,)), ((), ())), preferred_element_type=jnp.float32
    )
    high = part.astype(jnp.bfloat16).astype(jnp.float32)
    terms = jnp.concatenate([high, part - high], axis=1).astype(jnp.bfloat16)
    stores = []
    each = BLOCK // SPLITS
    for k in range(SPLITS):
        fetches[2 + k].wait()
        for d in range(k * each, (k + 1) * each):
            for head in range(KEY_VALUE_HEADS):
                columns = slice(head * HEAD_WIDTH, (head + 1) * HEAD_WIDTH)
                ready[head, d, :share] = held[d * share : (d + 1) * share, :, columns]
                for t in range(DECODE_STEPS):
                    ready[head, d, share + t // 2, t % 2, :] = terms[t]
        rows = pl.ds(k * each, each)
        stores.append(
            pltpu.make_async_copy(ready.at[:, rows], out.at[:, rows], sems.at[2 + SPLITS + k])
        )
        stores[-1].start()
    for store in stores:
        store.wait()


def attend_kernel(
    info, pos, pick, up0, up1, up2, up3, turn, cached, newest, out, query
):
    ups = (up0, up1, up2, up3)
    length = info[0]
    place = info[1]
    sums = jnp.dot(pick[...], cached[...], preferred_element_type=jnp.float32)
    half = HEAD_WIDTH // 2
    low = [
        sums[i * DECODE_STEPS : (i + 1) * DECODE_STEPS, :half]
        + sums[i * DECODE_STEPS : (i + 1) * DECODE_STEPS, half:]
        for i in range(2)
    ]
    low = jnp.concatenate(low, axis=1)
    rank = low.shape[1]
    high = low.astype(jnp.bfloat16).astype(jnp.float32)
    rest = low - high
    middle = rest.astype(jnp.bfloat16).astype(jnp.float32)
    terms = jnp.concatenate([high, middle, rest - middle, jnp.zeros_like(low)], axis=0).astype(
        jnp.bfloat16
    )
    cosine = turn[0]
    sine = turn[1]
    for j in range(BLOCK):
        step = up0.shape[0] // BLOCK_CORE
        start = pl.multiple_of((place ^ j) % BLOCK_CORE * step, 16)
        both = ups[j // BLOCK_CORE]
        extra = jnp.dot(
            terms, both[pl.ds(start, rank), :], preferred_element_type=jnp.float32
        )
        base = both[pl.ds(start + rank, 16), :].astype(jnp.float32)
        raw = ((base[8:12] + base[4:8]) + base[0:4]) + ((extra[8:12] + extra[4:8]) + extra[0:4])
        for i in range(2):
            head = raw[:, i * HEAD_WIDTH : (i + 1) * HEAD_WIDTH]
            row = (2 * j + i) * DECODE_STEPS
            query[row : row + DECODE_STEPS, :] = head * cosine + pltpu.roll(head, 64, 1) * sine
    queries = query[...].astype(jnp.bfloat16)
    scale = 1.0 / math.sqrt(HEAD_WIDTH)
    own = pl.ds(pl.multiple_of(info[2] * HEAD_WIDTH, HEAD_WIDTH), HEAD_WIDTH)
    token = newest[:, 0, 0, own].astype(jnp.float32)
    token = token * cosine + pltpu.roll(token, 64, 1) * sine
    blank = jnp.zeros((HEAD_WIDTH - DECODE_STEPS, HEAD_WIDTH), jnp.float32)
    fresh_key = jnp.concatenate([token, blank], axis=0).astype(jnp.bfloat16)
    fresh_value = jnp.concatenate(
        [newest[:, 0, 1, own].astype(jnp.float32), blank], axis=0
    ).astype(jnp.bfloat16)
    chunk = 768
    n_src = cached.shape[0] // chunk
    blocks = [slice(j * chunk, (j + 1) * chunk) for j in range(n_src)]
    row = lax.broadcasted_iota(jnp.int32, (ROWS, HEAD_WIDTH), 0)
    lane = lax.broadcasted_iota(jnp.int32, (ROWS, HEAD_WIDTH), 1)
    contract = (((1,), (1,)), ((), ()))
    masks = []
    scores = []
    for j in range(n_src):
        keys = cached[blocks[j], :]
        s = lax.dot_general(queries, keys, contract, preferred_element_type=jnp.float32)
        ok = jnp.broadcast_to(pos[:, blocks[j]] < length, s.shape)
        masks.append(ok)
        scores.append(jnp.where(ok, s * scale, MASKED))
    s = lax.dot_general(queries, fresh_key, contract, preferred_element_type=jnp.float32)
    ok = (lane <= lax.rem(row, DECODE_STEPS)) & (place == 0)
    masks.append(ok)
    scores.append(jnp.where(ok, s * scale, MASKED))
    top = jnp.max(scores[-1], axis=-1, keepdims=True)
    for s in scores[:-1]:
        top = jnp.maximum(top, jnp.max(s, axis=-1, keepdims=True))
    total = jnp.zeros_like(top)
    summed = jnp.zeros((ROWS, HEAD_WIDTH), jnp.float32)
    for j in range(n_src + 1):
        weight = jnp.where(masks[j], jnp.exp(scores[j] - top), 0.0)
        total = total + jnp.sum(weight, axis=-1, keepdims=True)
        if j < n_src:
            weight, values = pltpu.roll(weight, 1, 1), cached[blocks[j], :]
        else:
            values = fresh_value
        summed = summed + jnp.dot(
            weight.astype(jnp.bfloat16), values, preferred_element_type=jnp.float32
        )
    top = jnp.broadcast_to(top, summed.shape)
    total = jnp.broadcast_to(total, summed.shape)
    each = 2 * DECODE_STEPS
    for d in range(BLOCK):
        rows = slice(d * each, (d + 1) * each)
        for i, value in enumerate((summed, top, total)):
            out[place ^ d, i * each : (i + 1) * each, :] = value[rows, :]


def combine(parts):
    each = 2 * DECODE_STEPS
    summed, tops, totals = (
        [parts[d, i * each : (i + 1) * each] for d in range(BLOCK)] for i in range(3)
    )
    top = tops[0]
    for other in tops[1:]:
        top = jnp.maximum(top, other)
    above, below = 0.0, 0.0
    for d in range(BLOCK):
        factor = jnp.exp(tops[d] - top)
        above = above + summed[d] * factor
        below = below + totals[d] * factor
    whole = (above / below).astype(jnp.bfloat16)
    return jnp.concatenate([whole[:DECODE_STEPS], whole[DECODE_STEPS:]], axis=1)


def local(hidden, current_weight, down_factors, up_factors, cache, step_key_value, lengths):
    plane = ("y", "x", "core")
    block = ("x", "core")
    shard = lax.axis_index(plane)
    place = lax.axis_index(block)
    key_head = lax.axis_index(("role", "y"))
    rows = hidden.reshape(DECODE_STEPS, -1)
    down = down_factors[0, 0].T
    vmem = pl.BlockSpec(memory_space=pltpu.VMEM)
    smem = pl.BlockSpec(memory_space=pltpu.SMEM)
    everyone = ("role",) + plane
    share = cache.shape[1] // BLOCK
    sent = jax.ShapeDtypeStruct(
        (KEY_VALUE_HEADS, BLOCK, share + DECODE_STEPS // 2, 2, HEAD_WIDTH), cache.dtype
    )
    hbm = pl.BlockSpec(memory_space=pl.ANY)
    sent = pl.pallas_call(
        split_kernel,
        out_shape=sent,
        in_specs=[smem] + [hbm] * 3,
        out_specs=hbm,
        scratch_shapes=[
            pltpu.VMEM((rows.shape[0], down.shape[1]), rows.dtype),
            pltpu.VMEM(down.shape, down.dtype),
            pltpu.VMEM(cache.shape[1:], cache.dtype),
            pltpu.VMEM(sent.shape, sent.dtype),
            pltpu.SemaphoreType.DMA((2 + 2 * SPLITS,)),
        ],
        compiler_params=pltpu.CompilerParams(vmem_limit_bytes=58 * 2**20),
        name="split",
    )(shard[None].astype(jnp.int32), rows, down, cache[0])
    sent = sent.reshape((-1,) + sent.shape[2:])
    cached = lax.all_to_all(sent, everyone, 0, 0)
    rows_each = 2 * cached.shape[1]
    cached = cached.reshape(-1, HEAD_WIDTH)
    column = jnp.arange(cached.shape[0], dtype=jnp.int32)
    source, inner = column // rows_each, column % rows_each
    pos = source * cache.shape[1] + place * share + inner // 2
    pos = jnp.where((inner < 2 * share) & (inner % 2 == 0), pos, jnp.int32(2**30))[None]
    step = jnp.arange(16, dtype=jnp.int32)[:, None]
    new = source < lax.axis_size(everyone) // 2
    wanted = (inner >= 2 * share) & (inner - 2 * share == step % DECODE_STEPS)
    wanted = wanted & (step // DECODE_STEPS == jnp.where(new, 0, 1))
    pick = jnp.where(wanted, jnp.where(new, 1.0, -1.0), 0.0).astype(jnp.bfloat16)

    rows, sent = lax.optimization_barrier((rows, sent))
    base = jnp.dot(rows, current_weight, preferred_element_type=jnp.float32)
    high = lax.reduce_precision(base, 8, 7)
    middle = lax.reduce_precision(base - high, 8, 7)
    parts = [high, middle, base - high - middle, jnp.zeros_like(base)]
    parts = [term.astype(jnp.bfloat16) for term in parts]
    up = jnp.concatenate([up_factors.reshape(-1, up_factors.shape[-1])] + parts, axis=0)
    up = lax.all_gather(up, "core", axis=0, tiled=True)
    ups = [up] + [swapped(up, "x", m) for m in range(1, BLOCK_X)]

    steps_pos = lengths[None, :] + jnp.arange(DECODE_STEPS, dtype=jnp.int32)[:, None]
    cosine, sine = angles(steps_pos[:, 0])
    turn = jnp.stack(
        [
            jnp.concatenate([cosine, cosine], axis=-1),
            jnp.concatenate([-sine, sine], axis=-1),
        ]
    )
    info = jnp.stack([lengths[0], place, key_head]).astype(jnp.int32)

    parts = pl.pallas_call(
        attend_kernel,
        out_shape=jax.ShapeDtypeStruct((BLOCK, 6 * DECODE_STEPS, HEAD_WIDTH), jnp.float32),
        in_specs=[smem] + [vmem] * 9,
        out_specs=vmem,
        scratch_shapes=[pltpu.VMEM((ROWS, HEAD_WIDTH), jnp.float32)],
        compiler_params=pltpu.CompilerParams(vmem_limit_bytes=16 * 2**20),
        name="attend",
    )(info, pos, pick, *ups, turn, cached, step_key_value)
    parts = lax.all_to_all(parts, block, 0, 0)
    out = combine(parts)
    return out[:, None, :]


def solution(mesh):
    role, grp, tp = mesh.devices.shape
    finer = Mesh(
        mesh.devices.reshape(role, grp, tp // BLOCK, BLOCK_X, BLOCK_CORE),
        ("role", "grp", "y", "x", "core"),
    )
    tp = ("y", "x", "core")
    both = ("role",) + tp
    placed = (
        P(None, "grp", None),
        P(None, both),
        P("role", "grp", tp, None),
        P(None, "grp", None, both),
        P("grp", both, None, None),
        P(None, "grp", None, None),
        P("grp"),
    )
    return jax.shard_map(
        local, mesh=finer, in_specs=placed, out_specs=P(None, "grp", both), check_vma=False
    )
```
